128 devices in a mesh: orb: 8 (over y, core), pair: 16 (over x, z).
Axes of the slice: x: 4, y: 4, z: 4, core: 2. Of those that a mesh axis runs over, the one named last changes fastest.
Arguments:
- integrals: bfloat16 [16, 2048, 768], P('orb', 'pair'), may hold values from -0.75 to 0.75
- pno_maps: bfloat16 [384, 768, 384], P('orb'), may hold values from -0.21875 to 0.21875
- pair_orbs: int32 [384, 2], P('orb'), may hold values from 0 to 15
- pair_class: int32 [384], P(('orb', 'pair')), may hold values from 0 to 1
- orbital_energy: float32 [16], replicated, may hold values from -2 to -0.3
- pno_energy: float32 [384, 384], P(('orb', 'pair')), may hold values from 0.2 to 3
- amplitudes: float32 [384, 384, 384], P(('orb', 'pair')), may hold values from -2 to 2
Outputs:
- residual: float32 [384, 384, 384], P(('orb', 'pair'))
The draws below stay inside these ranges and needn't reach their ends.
Inputs may be any that keep to these rules, and one draw needn't show every extreme that they name: pair_class is 0 for a domain of 256 PNOs and 1 for one of 384. `pair_orbs`: orbital indices of each pair; i may equal j.
All inputs are finite; a program needn't handle non-finite values.
Results may differ from the reference program's by a relative error of at most 0.0017.
Values may be sent and summed in bfloat16 or wider, within the bound.
No kernel may reach another device: no remote copies, remote signals or barrier semaphores. Data moves between devices by JAX's collectives and lax.ppermute only.
A program may use at most 192 MiB of HBM per device.

```python
import jax
import jax.numpy as jnp
from jax import lax

Q = 2048
V = 768
NPNO = 384
NSMALL = 256
OCC = 16
PAIRS = 384


def plant(entries, rng, smallest, top_value):
    spot = [jax.random.randint(jax.random.fold_in(rng, axis), (), 0, length) for axis, length in enumerate(entries.shape)]
    main_axis = entries.shape.index(max(entries.shape))
    neighbour = spot[:main_axis] + [(spot[main_axis] + 1) % entries.shape[main_axis]] + spot[main_axis + 1:]
    return entries.at[tuple(spot)].set(smallest).at[tuple(neighbour)].set(top_value)


def levels(rng, dims, pieces, smallest, top_value):
    gain = 1.0
    for position, shards_of in pieces:
        draws = jax.random.uniform(jax.random.fold_in(jax.random.fold_in(rng, 6), position), (shards_of,), jnp.float32, smallest / len(pieces), top_value / len(pieces))
        gain = gain * jnp.repeat(jnp.exp(draws), dims[position] // shards_of).reshape((-1,) + (1,) * (len(dims) - 1 - position))
    return gain


def normal_values(rng, extent, deviation, limit, cuts=(), kind=jnp.bfloat16):
    drawn = jax.random.normal(rng, extent, jnp.float32) * deviation
    if len(cuts) > 0:
        drawn = levels(rng, extent, cuts, -0.22, 0.18) * drawn
    return jnp.clip(drawn, min=-limit, max=limit).astype(kind)


def setup_inputs(seed: int = 0) -> dict:
    arg_keys = jax.random.split(jax.random.key(seed), 8)
    integrals = normal_values(arg_keys[0], (OCC, Q, V), (Q // 32) ** -0.5, 0.75, ((0, 8), (1, 16)))
    pno_maps = normal_values(arg_keys[1], (PAIRS, V, NPNO), V ** -0.5, 0.21875, ((0, 8),))
    pair_orbs = plant(jax.random.randint(arg_keys[2], (PAIRS, 2), 0, OCC), jax.random.fold_in(arg_keys[2], 1), 0, OCC - 1).astype(jnp.int32)
    pair_class = plant(jax.random.randint(arg_keys[3], (PAIRS,), 0, 2), jax.random.fold_in(arg_keys[3], 1), 0, 1).astype(jnp.int32)
    orbital_energy = jnp.clip(jax.random.uniform(arg_keys[4], (OCC,), jnp.float32, -2.0, -0.3), -2.0, -0.3)
    pno_energy = jnp.clip(0.2 + 2.8 * jax.random.uniform(arg_keys[5], (PAIRS, NPNO), jnp.float32) ** levels(arg_keys[5], (PAIRS, NPNO), ((0, 128),), -0.2, 0.2), 0.2, 3.0)
    amplitudes = normal_values(arg_keys[6], (PAIRS, NPNO, NPNO), 0.3, 2.0, ((0, 128),), jnp.float32)
    return dict(integrals=integrals, pno_maps=pno_maps, pair_orbs=pair_orbs, pair_class=pair_class, orbital_energy=orbital_energy, pno_energy=pno_energy, amplitudes=amplitudes)


def pair_exchange(integrals, pair_orbs, pno_maps):
    def one_pair(items):
        orbs, dmap = items
        dmap = dmap.astype(jnp.float32)
        left = jnp.dot(integrals[orbs[0]].astype(jnp.float32), dmap, preferred_element_type=jnp.float32).astype(jnp.bfloat16)
        right = jnp.dot(integrals[orbs[1]].astype(jnp.float32), dmap, preferred_element_type=jnp.float32).astype(jnp.bfloat16)
        return lax.dot_general(left.astype(jnp.float32), right.astype(jnp.float32), (((0,), (0,)), ((), ())), preferred_element_type=jnp.float32)
    return lax.map(one_pair, (pair_orbs, pno_maps))


def reference(integrals, pno_maps, pair_orbs, pair_class, orbital_energy, pno_energy, amplitudes):
    exchange = pair_exchange(integrals, pair_orbs, pno_maps)
    sizes = NSMALL + pair_class * (NPNO - NSMALL)
    places = jnp.arange(NPNO, dtype=jnp.int32)
    keep = places[None, :] < sizes[:, None]
    window = keep[:, :, None] & keep[:, None, :]
    occupied = orbital_energy[pair_orbs[:, 0]] + orbital_energy[pair_orbs[:, 1]]
    denom = pno_energy[:, :, None] + pno_energy[:, None, :] - occupied[:, None, None]
    return jnp.where(window, exchange + denom * amplitudes, jnp.zeros_like(exchange))
```

```python
import functools

import jax
import jax.numpy as jnp
from jax import lax
from jax.experimental import pallas as pl
from jax.experimental.pallas import tpu as pltpu
from jax.sharding import PartitionSpec as P

NSMALL = 256
AXES = ("orb", "pair")
Y, C, X, Z = 4, 2, 4, 4
VMEM = 40 * 1024 * 1024


def flat(y, c, x, z):
    return (((y % Y) * C + c) * X + x % X) * Z + z % Z


def route(hop):
    return [
        (flat(y, c, x, z), flat(*hop(y, c, x, z)))
        for y in range(Y)
        for c in range(C)
        for x in range(X)
        for z in range(Z)
    ]


Y_ROUTE = route(lambda y, c, x, z: (y + 1 - 2 * c, c, x, z))
Z_ROUTE = route(lambda y, c, x, z: (y, c, x, z + 1 - 2 * c))
Y_FAR = route(lambda y, c, x, z: (y + 2, c, x, z))
Z_FAR = route(lambda y, c, x, z: (y, c, x, z + 2))
SWAP = route(lambda y, c, x, z: (y, 1 - c, x, z))
X_UP = route(lambda y, c, x, z: (y, c, x + 1, z))
X_DOWN = route(lambda y, c, x, z: (y, c, x - 1, z))


def send(value, way):
    return lax.ppermute(value, AXES, way)


def gather(own):
    other = send(own, SWAP)
    w = jnp.stack([own, other])
    ry, rz = send(w, Y_ROUTE), send(w, Z_ROUTE)
    ry2, rz2 = send(own, Y_FAR), send(own, Z_FAR)
    sy, sz = send(ry, SWAP), send(rz, SWAP)
    sy2, sz2 = send(ry2, SWAP), send(rz2, SWAP)
    rz3 = send(jnp.stack([ry[0, 0], ry[1, 0], sy[1, 0], sy[0, 0], ry2[0], sy2[0]]), Z_ROUTE)
    ry3 = send(jnp.stack([rz[0, 1], rz[1, 1], sz[1, 1], sz[0, 1], rz2[1], sz2[1]]), Y_ROUTE)
    rz5 = send(jnp.stack([rz3[0], rz3[2], rz3[4]]), Z_ROUTE)
    ry5 = send(jnp.stack([ry3[0], ry3[2], ry3[4]]), Y_ROUTE)
    sz3, sy3 = send(rz3, SWAP), send(ry3, SWAP)
    sz5, sy5 = send(rz5, SWAP), send(ry5, SWAP)
    pieces = dict(
        w=w, ry=ry, rz=rz, ry2=ry2, rz2=rz2, sy=sy, sz=sz, sy2=sy2, sz2=sz2,
        rz3=rz3, ry3=ry3, rz5=rz5, ry5=ry5, sz3=sz3, sy3=sy3, sz5=sz5, sy5=sy5,
    )
    flip = (0, 2, 1, 3)
    place = {}
    for l in range(2):
        for dc in range(2):
            place[0, 0, l, dc] = "w", (dc, l)
            for line in "yz":
                at = lambda d: (0, d) if line == "y" else (d, 0)
                place[(*at(1), l, dc)] = "r" + line, (dc, l)
                place[(*at(2), l, dc)] = "s" + line, (1 - dc, l)
                place[(*at(3), l, dc)] = "rs"[dc] + line + "2", (l,)
    for dc in range(2):
        for d in (1, 2, 3):
            for line, l in (("z", 0), ("y", 1)):
                at = lambda far: (far, d, l, dc) if line == "z" else (d, far, l, dc)
                place[at(1)] = "r" + line + "3", ((d - 1) * 2 + dc,)
                place[at(2)] = "s" + line + "3", ((flip[d] - 1) * 2 + 1 - dc,)
                place[at(3)] = ("r" + line + "5", (d - 1,)) if dc == 0 else ("s" + line + "5", (flip[d] - 1,))
    names = list(pieces)
    return list(pieces.values()), {k: (names.index(n), i) for k, (n, i) in place.items()}


def product(place, n_pieces, group, steps, rel, first, maps, pieces, buf, sems):
    step = pl.program_id(0)

    def copies(slot, side, r):
        found = []
        for dz in range(Z):
            piece, index = place[dz, r // 4, r // 2 % 2, r % 2]
            found.append(pltpu.make_async_copy(pieces[piece].at[index], buf.at[slot, side, dz], sems.at[slot, side, dz]))
        return found

    def fetch(which, slot):
        row = first[group] + which
        for side in range(2):
            mine = rel[row * 2 + side]
            for r in range(16):

                @pl.when(mine == r)
                def _(side=side, r=r):
                    for copy in copies(slot, side, r):
                        copy.start()

    slot = lax.rem(step, 2)

    @pl.when(step == 0)
    def _():
        fetch(0, 0)

    @pl.when(step + 1 < steps)
    def _():
        fetch(step + 1, 1 - slot)

    for side in range(2):
        for copy in copies(slot, side, 0):
            copy.wait()
    q, v = buf.shape[2] * buf.shape[3], buf.shape[4]
    dmap = maps[0]
    half = [
        jnp.dot(buf[slot, side].reshape(q, v), dmap, preferred_element_type=jnp.float32).astype(jnp.bfloat16)
        for side in range(2)
    ]
    return lax.dot_general(half[0], half[1], (((0,), (0,)), ((), ())), preferred_element_type=jnp.float32)


def partial_kernel(place, n, group, steps, rel, first, maps, *refs):
    pieces, (top, bottom), (buf, sems) = refs[:n], refs[n : n + 2], refs[n + 2 :]
    exchange = product(place, n, group, steps, rel, first, maps, pieces, buf, sems)
    rows = top.shape[1]
    top[0] = exchange[:rows].astype(top.dtype)
    bottom[0] = exchange[rows:].astype(bottom.dtype)


def own_kernel(place, n, group, steps, rel, first, maps, *refs):
    pieces, (high, low, occ, erow, ecol, amp), out, (buf, sems) = refs[:n], refs[n : n + 6], refs[n + 6], refs[n + 7 :]
    exchange = product(place, n, group, steps, rel, first, maps, pieces, buf, sems)
    denom = ecol[0] + erow[0] - occ[pl.program_id(0)]
    total = exchange + denom * amp[0]
    rows = high.shape[1]
    out[0, :rows] = total[:rows] + high[0].astype(jnp.float32)
    out[0, rows:] = total[rows:] + low[0].astype(jnp.float32)


def last_kernel(sizes, acc, high, low, out):
    p, h = pl.program_id(0), pl.program_id(1)
    size = sizes[p]
    rows, width = acc.shape[1:]
    a = lax.broadcasted_iota(jnp.int32, (rows, width), 0) + h * rows
    b = lax.broadcasted_iota(jnp.int32, (rows, width), 1)
    late = jnp.where(h == 0, high[0], low[0]).astype(jnp.float32)
    out[0] = jnp.where((a < size) & (b < size), acc[0] + late, 0.0)


def body(integrals, pno_maps, pair_orbs, pair_class, orbital_energy, pno_energy, amplitudes):
    groups = X * Z
    local_pairs, vectors, width = pno_maps.shape
    owned = local_pairs // groups
    rows = width // 2
    orb, spot = lax.axis_index("orb"), lax.axis_index("pair")
    y, c, x, z = orb // C, orb % C, spot // Z, spot % Z

    away = (pair_orbs // (2 * C) - y) % Y
    dy = jnp.where(away == 0, 0, jnp.where(away == 2, 3, jnp.where((away == 3) == (c == 0), 1, 2)))
    dc = (pair_orbs // 2 % C) ^ c
    rel = ((dy * 2 + pair_orbs % 2) * 2 + dc).reshape(-1).astype(jnp.int32)
    first = jnp.stack([owned * ((x + k) % X * Z + z) for k in range(X)]).astype(jnp.int32)

    pieces, place = gather(integrals)
    n = len(pieces)
    q = integrals.shape[1]
    anywhere = [pl.BlockSpec(memory_space=pl.ANY)] * n
    scratch = [
        pltpu.VMEM((2, 2, Z, q, vectors), jnp.bfloat16),
        pltpu.SemaphoreType.DMA((2, 2, Z)),
    ]
    flops = owned * (8 * Z * q * vectors * width // 2 + 2 * Z * q * width * width)
    cost = pl.CostEstimate(flops=flops, bytes_accessed=owned * (4 * Z * q * vectors + 2 * vectors * width + 4 * width * width), transcendentals=0)
    params = pltpu.CompilerParams(vmem_limit_bytes=VMEM)
    half = pl.BlockSpec((1, rows, width), lambda p, *_: (p, 0, 0))
    whole = pl.BlockSpec((1, width, width), lambda p, *_: (p, 0, 0))

    def maps_of(group):
        return pl.BlockSpec((1, vectors, width), lambda p, rel, first: (first[group] + p, 0, 0))

    def partial(group, kinds):
        return pl.pallas_call(
            functools.partial(partial_kernel, place, n, group, owned),
            grid_spec=pltpu.PrefetchScalarGridSpec(
                num_scalar_prefetch=2,
                grid=(owned,),
                in_specs=[maps_of(group), *anywhere],
                out_specs=[half, half],
                scratch_shapes=scratch,
            ),
            out_shape=[jax.ShapeDtypeStruct((owned, rows, width), kind) for kind in kinds],
            compiler_params=params,
            cost_estimate=cost,
        )(rel, first, pno_maps, *pieces)

    bf, f32 = jnp.bfloat16, jnp.float32
    far_top, far_bottom = partial(2, (bf, bf))
    far_top, far_bottom = send(far_top, X_UP), send(far_bottom, X_DOWN)
    up_top, up_bottom = partial(1, (f32, bf))
    up_bottom = send(up_bottom, X_UP)
    down_top, down_bottom = partial(3, (bf, f32))
    down_top = send(down_top, X_DOWN)
    up_top = send((up_top + far_top.astype(f32)).astype(bf), X_UP)
    down_bottom = send((down_bottom + far_bottom.astype(f32)).astype(bf), X_DOWN)

    start = spot * owned
    mine = lax.dynamic_slice_in_dim(pair_orbs, start, owned, 0)
    occupied = orbital_energy[mine[:, 0]] + orbital_energy[mine[:, 1]]
    sizes = NSMALL + pair_class * (width - NSMALL)
    acc = pl.pallas_call(
        functools.partial(own_kernel, place, n, 0, owned),
        grid_spec=pltpu.PrefetchScalarGridSpec(
            num_scalar_prefetch=2,
            grid=(owned,),
            in_specs=[
                maps_of(0),
                *anywhere,
                half,
                half,
                pl.BlockSpec(memory_space=pltpu.SMEM),
                pl.BlockSpec((1, 1, width), lambda p, *_: (p, 0, 0)),
                pl.BlockSpec((1, width, 1), lambda p, *_: (p, 0, 0)),
                whole,
            ],
            out_specs=whole,
            scratch_shapes=scratch,
        ),
        out_shape=jax.ShapeDtypeStruct((owned, width, width), f32),
        compiler_params=params,
        cost_estimate=cost,
    )(
        rel, first, pno_maps, *pieces, down_top, up_bottom, occupied,
        pno_energy[:, None, :], pno_energy[:, :, None], amplitudes,
    )
    part = pl.BlockSpec((1, rows, width), lambda p, h, *_: (p, h, 0))
    late = pl.BlockSpec((1, rows, width), lambda p, h, *_: (p, 0, 0))
    return pl.pallas_call(
        last_kernel,
        grid_spec=pltpu.PrefetchScalarGridSpec(
            num_scalar_prefetch=1, grid=(owned, 2), in_specs=[part, late, late], out_specs=part
        ),
        out_shape=jax.ShapeDtypeStruct((owned, width, width), f32),
        compiler_params=params,
    )(sizes, acc, up_top, down_bottom)


def solution(mesh):
    return jax.shard_map(
        body,
        mesh=mesh,
        in_specs=(
            P("orb", "pair", None),
            P("orb", None, None),
            P("orb", None),
            P(("orb", "pair")),
            P(),
            P(("orb", "pair"), None),
            P(("orb", "pair"), None, None),
        ),
        out_specs=P(("orb", "pair"), None, None),
        check_vma=False,
    )
```

```python
import functools

import jax
import jax.numpy as jnp
from jax import lax
from jax.experimental import pallas as pl
from jax.experimental.pallas import tpu as pltpu
from jax.sharding import PartitionSpec as P

NSMALL = 256
AXES = ("orb", "pair")
Y, C, X, Z = 4, 2, 4, 4
VMEM = 16 * 1024 * 1024


def flat(y, c, x, z):
    return (((y % Y) * C + c) * X + x % X) * Z + z % Z


def route(hop):
    return [
        (flat(y, c, x, z), flat(*hop(y, c, x, z)))
        for y in range(Y)
        for c in range(C)
        for x in range(X)
        for z in range(Z)
    ]


Y_ROUTE = route(lambda y, c, x, z: (y + 1 - 2 * c, c, x, z))
Z_ROUTE = route(lambda y, c, x, z: (y, c, x, z + 1 - 2 * c))
Y_FAR = route(lambda y, c, x, z: (y + 2, c, x, z))
Z_FAR = route(lambda y, c, x, z: (y, c, x, z + 2))
SWAP = route(lambda y, c, x, z: (y, 1 - c, x, z))
X_UP = route(lambda y, c, x, z: (y, c, x + 1, z))
X_DOWN = route(lambda y, c, x, z: (y, c, x - 1, z))


def send(value, way):
    return lax.ppermute(value, AXES, way)


def after(value, *others):
    return lax.optimization_barrier((value, *others))[0]


def gather(own):
    ry2, rz2 = send(own, Y_FAR), send(own, Z_FAR)
    other = send(own, SWAP)
    wa, wb = jnp.stack([own[0], other[0]]), jnp.stack([own[1], other[1]])
    ya, zb = send(wa, Y_ROUTE), send(wb, Z_ROUTE)
    yb, za = send(after(wb, ya, zb), Y_ROUTE), send(after(wa, ya, zb), Z_ROUTE)
    sya, szb, sry2, srz2 = (send(v, SWAP) for v in (ya, zb, ry2, rz2))
    on_z = jnp.stack([jnp.stack([ya[0], sya[1], ry2[0]]), jnp.stack([ya[1], sya[0], sry2[0]])])
    on_y = jnp.stack([jnp.stack([zb[0], szb[1], rz2[1]]), jnp.stack([zb[1], szb[0], srz2[1]])])
    rz3, ry3 = send(on_z, Z_ROUTE), send(on_y, Y_ROUTE)
    rz5, ry5 = send(rz3[0], Z_ROUTE), send(ry3[0], Y_ROUTE)
    syb, sza = send(after(yb, on_z, on_y), SWAP), send(after(za, on_z, on_y), SWAP)
    srz3, sry3, srz5, sry5 = (send(v, SWAP) for v in (rz3, ry3, rz5, ry5))
    return wa, wb, ya, sya, yb, syb, za, sza, zb, szb, ry2, sry2, rz2, srz2, rz3, srz3, rz5, srz5, ry3, sry3, ry5, sry5


FLIP = (0, 2, 1, 3)
N_PIECES = 22


def fetch(pieces, dy, l, dc, dst, sem):
    wa, wb, ya, sya, yb, syb, za, sza, zb, szb, ry2, sry2, rz2, srz2, rz3, srz3, rz5, srz5, ry3, sry3, ry5, sry5 = pieces
    def copy(src, dz):
        pltpu.make_async_copy(src, dst.at[dz], sem).start()

    flipped = jnp.where(dy == 3, 3, 3 - dy)

    @pl.when((l == 0) & (dy == 0))
    def _():
        copy(wa.at[dc], 0)
        copy(za.at[dc], 1)
        copy(sza.at[1 - dc], 2)

    @pl.when((l == 1) & (dy == 0))
    def _():
        copy(wb.at[dc], 0)
        copy(zb.at[dc], 1)
        copy(szb.at[1 - dc], 2)

    @pl.when((dy == 0) & (dc == 0))
    def _():
        copy(rz2.at[l], 3)

    @pl.when((dy == 0) & (dc == 1))
    def _():
        copy(srz2.at[l], 3)

    @pl.when((dy == 3) & (dc == 0))
    def _():
        copy(ry2.at[l], 0)

    @pl.when((dy == 3) & (dc == 1))
    def _():
        copy(sry2.at[l], 0)

    @pl.when((l == 0) & (dy != 0))
    def _():
        @pl.when(dy == 1)
        def _():
            copy(ya.at[dc], 0)

        @pl.when(dy == 2)
        def _():
            copy(sya.at[1 - dc], 0)

        copy(rz3.at[dc, dy - 1], 1)
        copy(srz3.at[1 - dc, flipped - 1], 2)

        @pl.when(dc == 0)
        def _():
            copy(rz5.at[dy - 1], 3)

        @pl.when(dc == 1)
        def _():
            copy(srz5.at[flipped - 1], 3)

    @pl.when((l == 1) & (dy == 1))
    def _():
        copy(yb.at[dc], 0)
        for dz in (1, 2, 3):
            copy(ry3.at[dc, dz - 1], dz)

    @pl.when((l == 1) & (dy == 2))
    def _():
        copy(syb.at[1 - dc], 0)
        for dz in (1, 2, 3):
            copy(sry3.at[1 - dc, FLIP[dz] - 1], dz)

    @pl.when((l == 1) & (dy == 3))
    def _():
        @pl.when(dc == 0)
        def _():
            for dz in (1, 2, 3):
                copy(ry5.at[dz - 1], dz)

        @pl.when(dc == 1)
        def _():
            for dz in (1, 2, 3):
                copy(sry5.at[FLIP[dz] - 1], dz)


def products(groups, here, orbs, maps, pieces, rows_of, dmaps, row_sems, sems, act):
    owned = dmaps.shape[0] // len(groups)
    pairs = owned * len(groups)

    def pair_of(n):
        row = here[2 + groups[0]] + n
        for i, group in enumerate(groups[1:], 1):
            row = jnp.where(n >= i * owned, here[2 + group] + n - i * owned, row)
        return row

    def start(n):
        pltpu.make_async_copy(maps.at[pair_of(n)], dmaps.at[n], sems.at[n]).start()

        @pl.loop(0, 2)
        def _(side):
            k = orbs[side, pair_of(n)]
            away = lax.rem(k // (2 * C) + Y - here[0], Y)
            near = jnp.where((away == 3) == (here[1] == 0), 1, 2)
            dy = jnp.where(away == 0, 0, jnp.where(away == 2, 3, near))
            slot = lax.rem(n, 2)
            fetch(pieces, dy, lax.rem(k, 2), lax.rem(k // 2 + here[1], 2), rows_of.at[slot, side], row_sems.at[slot, side])

    @pl.loop(0, pairs + 1)
    def _(n):
        @pl.when(n < pairs)
        def _():
            start(n)

        @pl.when(n > 0)
        def _():
            m = n - 1
            slot = lax.rem(m, 2)
            for side in range(2):
                rows = rows_of.at[slot, side]
                pltpu.make_async_copy(rows, rows, row_sems.at[slot, side]).wait()
            pltpu.make_async_copy(maps.at[0], dmaps.at[m], sems.at[m]).wait()
            q, v = rows_of.shape[2] * rows_of.shape[3], rows_of.shape[4]
            dmap = dmaps[m]
            half = [
                jnp.dot(rows_of[slot, side].reshape(q, v), dmap, preferred_element_type=jnp.float32).astype(jnp.bfloat16)
                for side in range(2)
            ]
            exchange = lax.dot_general(half[0], half[1], (((0,), (0,)), ((), ())), preferred_element_type=jnp.float32)
            for i, group in enumerate(groups):
                if len(groups) == 1:
                    act(group, m, exchange)
                else:

                    @pl.when((m >= i * owned) & (m < (i + 1) * owned))
                    def _(i=i, group=group):
                        act(group, m - i * owned, exchange)


def partial_kernel(groups, here, orbs, maps, *refs):
    pieces, outs, scratch = refs[:N_PIECES], refs[N_PIECES : N_PIECES + 2 * len(groups)], refs[-4:]

    def act(group, p, exchange):
        top, bottom = outs[2 * groups.index(group) :][:2]
        rows = top.shape[1]
        top[p] = exchange[:rows].astype(top.dtype)
        bottom[p] = exchange[rows:].astype(bottom.dtype)

    products(groups, here, orbs, maps, pieces, *scratch, act)


def own_kernel(here, orbs, maps, *refs):
    pieces, (high, low, orbital_energy, energy, amp, out) = refs[:N_PIECES], refs[N_PIECES : N_PIECES + 6]

    def act(_, p, exchange):
        row = here[2] + p
        occupied = orbital_energy[orbs[0, row]] + orbital_energy[orbs[1, row]]
        along = jnp.broadcast_to(energy[pl.ds(p, 1), :], exchange.shape)
        total = exchange + (along.T + along - occupied) * amp[p]
        rows = high.shape[1]
        out[p, :rows] = total[:rows] + high[p].astype(jnp.float32)
        out[p, rows:] = total[rows:] + low[p].astype(jnp.float32)

    products((0,), here, orbs, maps, pieces, *refs[-4:], act)


def last_kernel(kinds, acc, high, low, out, staged, sems):
    owned, rows, width = high.shape
    b = lax.broadcasted_iota(jnp.int32, (rows, width), 1)
    copies = []
    for p in range(owned):
        size = NSMALL + kinds[p] * (width - NSMALL)
        for begin, late in ((0, high), (rows, low)):
            a = lax.broadcasted_iota(jnp.int32, (rows, width), 0) + begin
            part = pl.ds(begin, rows)
            staged[p, part] = jnp.where((a < size) & (b < size), acc[p, part] + late[p].astype(jnp.float32), 0.0)
        copies.append(pltpu.make_async_copy(staged.at[p], out.at[p], sems.at[p]))
        copies[-1].start()
    for copy in copies:
        copy.wait()


def body(integrals, pno_maps, pair_orbs, pair_class, orbital_energy, pno_energy, amplitudes):
    local_pairs, vectors, width = pno_maps.shape
    owned = local_pairs // (X * Z)
    rows = width // 2
    orb, spot = lax.axis_index("orb"), lax.axis_index("pair")
    x, z = spot // Z, spot % Z
    here = jnp.stack([orb // C, orb % C] + [owned * ((x + k) % X * Z + z) for k in range(X)]).astype(jnp.int32)
    orbs = pair_orbs.T
    pno_maps = pltpu.with_memory_space_constraint(pno_maps, pltpu.HBM)

    pieces = [pltpu.with_memory_space_constraint(piece, pltpu.HBM) for piece in gather(integrals)]
    q = integrals.shape[1]
    smem, vmem, anywhere = (pl.BlockSpec(memory_space=m) for m in (pltpu.SMEM, pltpu.VMEM, pl.ANY))
    params = pltpu.CompilerParams(vmem_limit_bytes=VMEM)
    bf, f32 = jnp.bfloat16, jnp.float32

    def call(kernel, n_groups, shapes, *late):
        pairs = owned * n_groups
        return pl.pallas_call(
            kernel,
            in_specs=[smem, smem, anywhere] + [anywhere] * N_PIECES + [vmem, vmem, smem, vmem, vmem][: len(late)],
            out_specs=[vmem] * len(shapes),
            out_shape=shapes,
            scratch_shapes=[
                pltpu.VMEM((2, 2, Z, q, vectors), bf),
                pltpu.VMEM((pairs, vectors, width), bf),
                pltpu.SemaphoreType.DMA((2, 2)),
                pltpu.SemaphoreType.DMA((pairs,)),
            ],
            compiler_params=params,
            cost_estimate=pl.CostEstimate(
                flops=pairs * (4 * Z * q * vectors * width + 2 * Z * q * width * width),
                bytes_accessed=pairs * (2 * vectors * width + 4 * width * width),
                transcendentals=0,
            ),
        )(here, orbs, pno_maps, *pieces, *late)

    def partial(groups, *kinds):
        shapes = [jax.ShapeDtypeStruct((owned, rows, width), kind) for kind in kinds]
        return call(functools.partial(partial_kernel, groups), len(groups), shapes)

    far_top, far_bottom = partial((2,), bf, bf)
    far_top, far_bottom = send(far_top, X_UP), send(far_bottom, X_DOWN)
    up_top, up_bottom = partial((1,), f32, bf)
    up_bottom = send(up_bottom, X_UP)
    down_top, down_bottom = partial((3,), bf, f32)
    down_top = send(down_top, X_DOWN)
    up_top = send((up_top + far_top.astype(f32)).astype(bf), X_UP)
    down_bottom = send((down_bottom + far_bottom.astype(f32)).astype(bf), X_DOWN)

    whole = jax.ShapeDtypeStruct((owned, width, width), f32)
    (acc,) = call(own_kernel, 1, [whole], down_top, up_bottom, orbital_energy, pno_energy, amplitudes)
    return pl.pallas_call(
        last_kernel,
        in_specs=[smem, vmem, vmem, vmem],
        out_specs=anywhere,
        out_shape=whole,
        scratch_shapes=[pltpu.VMEM((owned, width, width), f32), pltpu.SemaphoreType.DMA((owned,))],
        compiler_params=params,
    )(pair_class, acc, up_top, down_bottom)


def solution(mesh):
    return jax.shard_map(
        body,
        mesh=mesh,
        in_specs=(
            P("orb", "pair", None),
            P("orb", None, None),
            P("orb", None),
            P(("orb", "pair")),
            P(),
            P(("orb", "pair"), None),
            P(("orb", "pair"), None, None),
        ),
        out_specs=P(("orb", "pair"), None, None),
        check_vma=False,
    )
```

```python
import functools

import jax
import jax.numpy as jnp
from jax import lax
from jax.experimental import pallas as pl
from jax.experimental.pallas import tpu as pltpu
from jax.sharding import PartitionSpec as P

NSMALL = 256
AXES = ("orb", "pair")
Y, C, X, Z = 4, 2, 4, 4
VMEM = 16 * 1024 * 1024


def flat(y, c, x, z):
    return (((y % Y) * C + c) * X + x % X) * Z + z % Z


def route(hop):
    return [
        (flat(y, c, x, z), flat(*hop(y, c, x, z)))
        for y in range(Y)
        for c in range(C)
        for x in range(X)
        for z in range(Z)
    ]


Y_ROUTE = route(lambda y, c, x, z: (y + 1 - 2 * c, c, x, z))
Z_ROUTE = route(lambda y, c, x, z: (y, c, x, z + 1 - 2 * c))
Y_FAR = route(lambda y, c, x, z: (y + 2, c, x, z))
Z_FAR = route(lambda y, c, x, z: (y, c, x, z + 2))
SWAP = route(lambda y, c, x, z: (y, 1 - c, x, z))
X_AHEAD = route(lambda y, c, x, z: (y, c, x + 1 - 2 * c, z))
X_BEHIND = route(lambda y, c, x, z: (y, c, x - 1 + 2 * c, z))


def send(value, way):
    return lax.ppermute(value, AXES, way)


def after(value, *others):
    return lax.optimization_barrier((value, *others))[0]


def gather(own):
    ry2, rz2 = send(own, Y_FAR), send(own, Z_FAR)
    other = send(own, SWAP)
    wa, wb = jnp.stack([own[0], other[0]]), jnp.stack([own[1], other[1]])
    ya, zb = send(wa, Y_ROUTE), send(wb, Z_ROUTE)
    yb, za = send(after(wb, ya, zb), Y_ROUTE), send(after(wa, ya, zb), Z_ROUTE)
    sya, szb, sry2, srz2 = (send(v, SWAP) for v in (ya, zb, ry2, rz2))
    on_z = jnp.stack([jnp.stack([ya[0], sya[1], ry2[0]]), jnp.stack([ya[1], sya[0], sry2[0]])])
    on_y = jnp.stack([jnp.stack([zb[0], szb[1], rz2[1]]), jnp.stack([zb[1], szb[0], srz2[1]])])
    rz3, ry3 = send(on_z, Z_ROUTE), send(on_y, Y_ROUTE)
    rz5, ry5 = send(rz3[0], Z_ROUTE), send(ry3[0], Y_ROUTE)
    syb, sza = send(after(yb, on_z, on_y), SWAP), send(after(za, on_z, on_y), SWAP)
    srz3, sry3, srz5, sry5 = (send(v, SWAP) for v in (rz3, ry3, rz5, ry5))
    return wa, wb, ya, sya, yb, syb, za, sza, zb, szb, ry2, sry2, rz2, srz2, rz3, srz3, rz5, srz5, ry3, sry3, ry5, sry5


FLIP = (0, 2, 1, 3)
N_PIECES = 22


def fetch(pieces, dy, l, dc, dst, sem):
    wa, wb, ya, sya, yb, syb, za, sza, zb, szb, ry2, sry2, rz2, srz2, rz3, srz3, rz5, srz5, ry3, sry3, ry5, sry5 = pieces
    def copy(src, dz):
        pltpu.make_async_copy(src, dst.at[dz], sem).start()

    flipped = jnp.where(dy == 3, 3, 3 - dy)

    @pl.when((l == 0) & (dy == 0))
    def _():
        copy(wa.at[dc], 0)
        copy(za.at[dc], 1)
        copy(sza.at[1 - dc], 2)

    @pl.when((l == 1) & (dy == 0))
    def _():
        copy(wb.at[dc], 0)
        copy(zb.at[dc], 1)
        copy(szb.at[1 - dc], 2)

    @pl.when((dy == 0) & (dc == 0))
    def _():
        copy(rz2.at[l], 3)

    @pl.when((dy == 0) & (dc == 1))
    def _():
        copy(srz2.at[l], 3)

    @pl.when((dy == 3) & (dc == 0))
    def _():
        copy(ry2.at[l], 0)

    @pl.when((dy == 3) & (dc == 1))
    def _():
        copy(sry2.at[l], 0)

    @pl.when((l == 0) & (dy != 0))
    def _():
        @pl.when(dy == 1)
        def _():
            copy(ya.at[dc], 0)

        @pl.when(dy == 2)
        def _():
            copy(sya.at[1 - dc], 0)

        copy(rz3.at[dc, dy - 1], 1)
        copy(srz3.at[1 - dc, flipped - 1], 2)

        @pl.when(dc == 0)
        def _():
            copy(rz5.at[dy - 1], 3)

        @pl.when(dc == 1)
        def _():
            copy(srz5.at[flipped - 1], 3)

    @pl.when((l == 1) & (dy == 1))
    def _():
        copy(yb.at[dc], 0)
        for dz in (1, 2, 3):
            copy(ry3.at[dc, dz - 1], dz)

    @pl.when((l == 1) & (dy == 2))
    def _():
        copy(syb.at[1 - dc], 0)
        for dz in (1, 2, 3):
            copy(sry3.at[1 - dc, FLIP[dz] - 1], dz)

    @pl.when((l == 1) & (dy == 3))
    def _():
        @pl.when(dc == 0)
        def _():
            for dz in (1, 2, 3):
                copy(ry5.at[dz - 1], dz)

        @pl.when(dc == 1)
        def _():
            for dz in (1, 2, 3):
                copy(sry5.at[FLIP[dz] - 1], dz)


def sweep(group, here, orbs, maps, pieces, scratch, act):
    rows_of, dmaps, row_sems, map_sems = scratch
    pairs = orbs.shape[1] // (X * Z)

    def start(p):
        row = here[2 + group] + p
        slot = lax.rem(p, 2)
        pltpu.make_async_copy(maps.at[row], dmaps.at[slot], map_sems.at[slot]).start()

        @pl.loop(0, 2)
        def _(side):
            k = orbs[side, row]
            away = lax.rem(k // (2 * C) + Y - here[0], Y)
            near = jnp.where((away == 3) == (here[1] == 0), 1, 2)
            dy = jnp.where(away == 0, 0, jnp.where(away == 2, 3, near))
            dc = lax.rem(k // 2 + here[1], 2)
            fetch(pieces, dy, lax.rem(k, 2), dc, rows_of.at[slot, side], row_sems.at[slot, side])

    @pl.loop(0, pairs + 1)
    def _(n):
        @pl.when(n < pairs)
        def _():
            start(n)

        @pl.when(n > 0)
        def _():
            p = n - 1
            slot = lax.rem(p, 2)
            pltpu.make_async_copy(dmaps.at[slot], dmaps.at[slot], map_sems.at[slot]).wait()
            for side in range(2):
                rows = rows_of.at[slot, side]
                pltpu.make_async_copy(rows, rows, row_sems.at[slot, side]).wait()
            q, v = rows_of.shape[2] * rows_of.shape[3], rows_of.shape[4]
            act(p, dmaps[slot], *(rows_of[slot, side].reshape(q, v) for side in range(2)))


def left_t(dmap, rows):
    product = lax.dot_general(dmap, rows, (((0,), (1,)), ((), ())), preferred_element_type=jnp.float32)
    return product.astype(jnp.bfloat16)


def right(dmap, rows):
    return jnp.dot(rows, dmap, preferred_element_type=jnp.float32).astype(jnp.bfloat16)


def meet(lt, r):
    return jnp.dot(lt, r, preferred_element_type=jnp.float32)


def partial_kernel(group, here, orbs, maps, *refs):
    pieces, (top, bottom), scratch = refs[:N_PIECES], refs[N_PIECES : N_PIECES + 2], refs[N_PIECES + 2 :]
    rows = top.shape[1]

    def act(p, dmap, left_rows, right_rows):
        exchange = meet(left_t(dmap, left_rows), right(dmap, right_rows))
        top[p] = exchange[:rows].astype(top.dtype)
        bottom[p] = exchange[rows:].astype(bottom.dtype)

    sweep(group, here, orbs, maps, pieces, scratch, act)


def own_kernel(here, orbs, maps, *refs):
    pieces, (orbital_energy, energy, amp, out) = refs[:N_PIECES], refs[N_PIECES : N_PIECES + 4]

    def act(p, dmap, left_rows, right_rows):
        row = here[2] + p
        occupied = orbital_energy[orbs[0, row]] + orbital_energy[orbs[1, row]]
        exchange = meet(left_t(dmap, left_rows), right(dmap, right_rows))
        along = jnp.broadcast_to(energy[pl.ds(p, 1), :], exchange.shape)
        out[p] = exchange + (along.T + along - occupied) * amp[p]

    sweep(0, here, orbs, maps, pieces, refs[N_PIECES + 4 :], act)


def last_kernel(kinds, acc, up_top, up_bottom, down_top, down_bottom, out, staged, sems):
    owned, rows, width = up_top.shape
    b = lax.broadcasted_iota(jnp.int32, (rows, width), 1)
    copies = []
    for p in range(owned):
        size = NSMALL + kinds[p] * (width - NSMALL)
        for begin, near, late in ((0, down_top, up_top), (rows, up_bottom, down_bottom)):
            a = lax.broadcasted_iota(jnp.int32, (rows, width), 0) + begin
            part = pl.ds(begin, rows)
            total = acc[p, part] + near[p].astype(jnp.float32) + late[p].astype(jnp.float32)
            staged[p, part] = jnp.where((a < size) & (b < size), total, 0.0)
        copies.append(pltpu.make_async_copy(staged.at[p], out.at[p], sems.at[p]))
        copies[-1].start()
    for copy in copies:
        copy.wait()


def body(integrals, pno_maps, pair_orbs, pair_class, orbital_energy, pno_energy, amplitudes):
    local_pairs, vectors, width = pno_maps.shape
    owned = local_pairs // (X * Z)
    rows = width // 2
    orb, spot = lax.axis_index("orb"), lax.axis_index("pair")
    x, z = spot // Z, spot % Z
    c = orb % C
    ahead = 1 - 2 * c
    here = jnp.stack([orb // C, c] + [owned * ((x + k * ahead + 4 * X) % X * Z + z) for k in range(X)]).astype(jnp.int32)
    orbs = pair_orbs.T
    pno_maps = pltpu.with_memory_space_constraint(pno_maps, pltpu.HBM)

    pieces = [pltpu.with_memory_space_constraint(piece, pltpu.HBM) for piece in gather(integrals)]
    q = integrals.shape[1]
    smem, vmem, anywhere = (pl.BlockSpec(memory_space=m) for m in (pltpu.SMEM, pltpu.VMEM, pl.ANY))
    params = pltpu.CompilerParams(vmem_limit_bytes=VMEM)
    bf, f32 = jnp.bfloat16, jnp.float32

    def call(kernel, *shapes, more_specs=(), more=()):
        return pl.pallas_call(
            kernel,
            in_specs=[smem, smem, anywhere] + [anywhere] * N_PIECES + list(more_specs),
            out_specs=[vmem] * len(shapes),
            out_shape=shapes,
            scratch_shapes=[
                pltpu.VMEM((2, 2, Z, q, vectors), bf),
                pltpu.VMEM((2, vectors, width), bf),
                pltpu.SemaphoreType.DMA((2, 2)),
                pltpu.SemaphoreType.DMA((2,)),
            ],
            compiler_params=params,
            cost_estimate=pl.CostEstimate(
                flops=owned * (4 * Z * q * vectors * width + 2 * Z * q * width * width),
                bytes_accessed=owned * (4 * Z * q * vectors + 2 * vectors * width + 4 * width * width),
                transcendentals=0,
            ),
        )(here, orbs, pno_maps, *pieces, *more)

    def partial(group, *kinds):
        shapes = [jax.ShapeDtypeStruct((owned, rows, width), kind) for kind in kinds]
        return call(functools.partial(partial_kernel, group), *shapes)

    far_top, far_bottom = partial(2, bf, bf)
    far_top, far_bottom = send(far_top, X_AHEAD), send(far_bottom, X_BEHIND)
    up_top, up_bottom = partial(1, f32, bf)
    up_bottom = send(up_bottom, X_AHEAD)
    down_top, down_bottom = partial(3, bf, f32)
    down_top = send(down_top, X_BEHIND)
    up_top = send((up_top + far_top.astype(f32)).astype(bf), X_AHEAD)
    down_bottom = send((down_bottom + far_bottom.astype(f32)).astype(bf), X_BEHIND)

    whole = jax.ShapeDtypeStruct((owned, width, width), f32)
    (acc,) = call(own_kernel, whole, more_specs=[smem, vmem, vmem], more=(orbital_energy, pno_energy, amplitudes))
    return pl.pallas_call(
        last_kernel,
        in_specs=[smem, vmem, vmem, vmem, vmem, vmem],
        out_specs=anywhere,
        out_shape=whole,
        scratch_shapes=[pltpu.VMEM((owned, width, width), f32), pltpu.SemaphoreType.DMA((owned,))],
        compiler_params=params,
    )(pair_class, acc, up_top, up_bottom, down_top, down_bottom)


def solution(mesh):
    return jax.shard_map(
        body,
        mesh=mesh,
        in_specs=(
            P("orb", "pair", None),
            P("orb", None, None),
            P("orb", None),
            P(("orb", "pair")),
            P(),
            P(("orb", "pair"), None),
            P(("orb", "pair"), None, None),
        ),
        out_specs=P(("orb", "pair"), None, None),
        check_vma=False,
    )
```

```python
import functools

import jax
import jax.numpy as jnp
from jax import lax
from jax.experimental import pallas as pl
from jax.experimental.pallas import tpu as pltpu
from jax.sharding import PartitionSpec as P

NSMALL = 256
AXES = ("orb", "pair")
Y, C, X, Z = 4, 2, 4, 4
VMEM = 16 * 1024 * 1024


def flat(y, c, x, z):
    return (((y % Y) * C + c) * X + x % X) * Z + z % Z


def route(hop):
    return [
        (flat(y, c, x, z), flat(*hop(y, c, x, z)))
        for y in range(Y)
        for c in range(C)
        for x in range(X)
        for z in range(Z)
    ]


Y_ROUTE = route(lambda y, c, x, z: (y + 1 - 2 * c, c, x, z))
Z_ROUTE = route(lambda y, c, x, z: (y, c, x, z + 1 - 2 * c))
Y_FAR = route(lambda y, c, x, z: (y + 2, c, x, z))
Z_FAR = route(lambda y, c, x, z: (y, c, x, z + 2))
SWAP = route(lambda y, c, x, z: (y, 1 - c, x, z))
X_AHEAD = route(lambda y, c, x, z: (y, c, x + 1 - 2 * c, z))
X_BEHIND = route(lambda y, c, x, z: (y, c, x - 1 + 2 * c, z))


def send(value, way):
    return lax.ppermute(value, AXES, way)


def after(value, *others):
    return lax.optimization_barrier((value, *others))[0]


def gather(own):
    rz2 = send(own, Z_FAR)
    other = send(own, SWAP)
    wb = jnp.stack([own[1], other[1]])
    ry2 = send(own, Y_FAR)
    srz2 = send(rz2, SWAP)
    zb = send(wb, Z_ROUTE)
    sry2 = send(ry2, SWAP)
    wa = jnp.stack([own[0], other[0]])
    ya = send(wa, Y_ROUTE)
    za = send(after(wa, ya, zb), Z_ROUTE)
    yb = send(after(wb, ya, zb), Y_ROUTE)
    sya = send(ya, SWAP)
    on_z = jnp.stack([jnp.stack([ya[0], sya[1], ry2[0]]), jnp.stack([ya[1], sya[0], sry2[0]])])
    rz3 = send(on_z, Z_ROUTE)
    srz3 = send(rz3, SWAP)
    rz5 = send(rz3[0], Z_ROUTE)
    srz5 = send(rz5, SWAP)
    szb = send(zb, SWAP)
    on_y = jnp.stack([jnp.stack([zb[0], szb[1], rz2[1]]), jnp.stack([zb[1], szb[0], srz2[1]])])
    ry3 = send(on_y, Y_ROUTE)
    sry3 = send(ry3, SWAP)
    leaf = send(jnp.stack([after(yb, on_z, on_y), za]), SWAP)
    ry5 = send(ry3[0], Y_ROUTE)
    sry5 = send(ry5, SWAP)
    return wa, wb, ya, sya, yb, za, leaf, zb, szb, ry2, sry2, rz2, srz2, rz3, srz3, rz5, srz5, ry3, sry3, ry5, sry5


FLIP = (0, 2, 1, 3)
N_PIECES = 21


def fetch(pieces, dy, l, dc, dst, sem):
    wa, wb, ya, sya, yb, za, leaf, zb, szb, ry2, sry2, rz2, srz2, rz3, srz3, rz5, srz5, ry3, sry3, ry5, sry5 = pieces
    syb, sza = leaf.at[0], leaf.at[1]
    def copy(src, dz):
        pltpu.make_async_copy(src, dst.at[dz], sem).start()

    flipped = jnp.where(dy == 3, 3, 3 - dy)

    @pl.when((l == 0) & (dy == 0))
    def _():
        copy(wa.at[dc], 0)
        copy(za.at[dc], 1)
        copy(sza.at[1 - dc], 2)

    @pl.when((l == 1) & (dy == 0))
    def _():
        copy(wb.at[dc], 0)
        copy(zb.at[dc], 1)
        copy(szb.at[1 - dc], 2)

    @pl.when((dy == 0) & (dc == 0))
    def _():
        copy(rz2.at[l], 3)

    @pl.when((dy == 0) & (dc == 1))
    def _():
        copy(srz2.at[l], 3)

    @pl.when((dy == 3) & (dc == 0))
    def _():
        copy(ry2.at[l], 0)

    @pl.when((dy == 3) & (dc == 1))
    def _():
        copy(sry2.at[l], 0)

    @pl.when((l == 0) & (dy != 0))
    def _():
        @pl.when(dy == 1)
        def _():
            copy(ya.at[dc], 0)

        @pl.when(dy == 2)
        def _():
            copy(sya.at[1 - dc], 0)

        copy(rz3.at[dc, dy - 1], 1)
        copy(srz3.at[1 - dc, flipped - 1], 2)

        @pl.when(dc == 0)
        def _():
            copy(rz5.at[dy - 1], 3)

        @pl.when(dc == 1)
        def _():
            copy(srz5.at[flipped - 1], 3)

    @pl.when((l == 1) & (dy == 1))
    def _():
        copy(yb.at[dc], 0)
        for dz in (1, 2, 3):
            copy(ry3.at[dc, dz - 1], dz)

    @pl.when((l == 1) & (dy == 2))
    def _():
        copy(syb.at[1 - dc], 0)
        for dz in (1, 2, 3):
            copy(sry3.at[1 - dc, FLIP[dz] - 1], dz)

    @pl.when((l == 1) & (dy == 3))
    def _():
        @pl.when(dc == 0)
        def _():
            for dz in (1, 2, 3):
                copy(ry5.at[dz - 1], dz)

        @pl.when(dc == 1)
        def _():
            for dz in (1, 2, 3):
                copy(sry5.at[FLIP[dz] - 1], dz)


def sweep(group, here, orbs, maps, pieces, scratch, act):
    rows_of, dmaps, row_sems, map_sems = scratch
    pairs = orbs.shape[1] // (X * Z)

    def start(p):
        row = here[2 + group] + p
        slot = lax.rem(p, 2)
        pltpu.make_async_copy(maps.at[row], dmaps.at[slot], map_sems.at[slot]).start()

        @pl.loop(0, 2)
        def _(side):
            k = orbs[side, row]
            away = lax.rem(k // (2 * C) + Y - here[0], Y)
            near = jnp.where((away == 3) == (here[1] == 0), 1, 2)
            dy = jnp.where(away == 0, 0, jnp.where(away == 2, 3, near))
            dc = lax.rem(k // 2 + here[1], 2)
            fetch(pieces, dy, lax.rem(k, 2), dc, rows_of.at[slot, side], row_sems.at[slot, side])

    @pl.loop(0, pairs + 1)
    def _(n):
        @pl.when(n < pairs)
        def _():
            start(n)

        @pl.when(n > 0)
        def _():
            p = n - 1
            slot = lax.rem(p, 2)
            pltpu.make_async_copy(dmaps.at[slot], dmaps.at[slot], map_sems.at[slot]).wait()
            for side in range(2):
                rows = rows_of.at[slot, side]
                pltpu.make_async_copy(rows, rows, row_sems.at[slot, side]).wait()
            q, v = rows_of.shape[2] * rows_of.shape[3], rows_of.shape[4]
            act(p, dmaps[slot], *(rows_of[slot, side].reshape(q, v) for side in range(2)))


def left_t(dmap, rows):
    product = lax.dot_general(dmap, rows, (((0,), (1,)), ((), ())), preferred_element_type=jnp.float32)
    return product.astype(jnp.bfloat16)


def right(dmap, rows):
    return jnp.dot(rows, dmap, preferred_element_type=jnp.float32).astype(jnp.bfloat16)


def meet(lt, r):
    return jnp.dot(lt, r, preferred_element_type=jnp.float32)


def partial_kernel(group, here, orbs, maps, *refs):
    pieces, (top, bottom), scratch = refs[:N_PIECES], refs[N_PIECES : N_PIECES + 2], refs[N_PIECES + 2 :]
    rows = top.shape[1]

    def act(p, dmap, left_rows, right_rows):
        exchange = meet(left_t(dmap, left_rows), right(dmap, right_rows))
        top[p] = exchange[:rows].astype(top.dtype)
        bottom[p] = exchange[rows:].astype(bottom.dtype)

    sweep(group, here, orbs, maps, pieces, scratch, act)


def own_kernel(here, orbs, maps, *refs):
    pieces, (orbital_energy, energy, amp, out) = refs[:N_PIECES], refs[N_PIECES : N_PIECES + 4]

    def act(p, dmap, left_rows, right_rows):
        row = here[2] + p
        occupied = orbital_energy[orbs[0, row]] + orbital_energy[orbs[1, row]]
        exchange = meet(left_t(dmap, left_rows), right(dmap, right_rows))
        along = jnp.broadcast_to(energy[pl.ds(p, 1), :], exchange.shape)
        out[p] = exchange + (along.T + along - occupied) * amp[p]

    sweep(0, here, orbs, maps, pieces, refs[N_PIECES + 4 :], act)


def last_kernel(kinds, acc, up_top, up_bottom, down_top, down_bottom, out, staged, sems):
    owned, rows, width = up_top.shape
    b = lax.broadcasted_iota(jnp.int32, (rows, width), 1)
    copies = []
    for p in range(owned):
        size = NSMALL + kinds[p] * (width - NSMALL)
        for begin, near, late in ((0, down_top, up_top), (rows, up_bottom, down_bottom)):
            a = lax.broadcasted_iota(jnp.int32, (rows, width), 0) + begin
            part = pl.ds(begin, rows)
            total = acc[p, part] + near[p].astype(jnp.float32) + late[p].astype(jnp.float32)
            staged[p, part] = jnp.where((a < size) & (b < size), total, 0.0)
        copies.append(pltpu.make_async_copy(staged.at[p], out.at[p], sems.at[p]))
        copies[-1].start()
    for copy in copies:
        copy.wait()


def body(integrals, pno_maps, pair_orbs, pair_class, orbital_energy, pno_energy, amplitudes):
    local_pairs, vectors, width = pno_maps.shape
    owned = local_pairs // (X * Z)
    rows = width // 2
    orb, spot = lax.axis_index("orb"), lax.axis_index("pair")
    x, z = spot // Z, spot % Z
    c = orb % C
    ahead = 1 - 2 * c
    here = jnp.stack([orb // C, c] + [owned * ((x + k * ahead + 4 * X) % X * Z + z) for k in range(X)]).astype(jnp.int32)
    orbs = pair_orbs.T
    pno_maps = pltpu.with_memory_space_constraint(pno_maps, pltpu.HBM)

    pieces = [pltpu.with_memory_space_constraint(piece, pltpu.HBM) for piece in gather(integrals)]
    q = integrals.shape[1]
    smem, vmem, anywhere = (pl.BlockSpec(memory_space=m) for m in (pltpu.SMEM, pltpu.VMEM, pl.ANY))
    params = pltpu.CompilerParams(vmem_limit_bytes=VMEM)
    bf, f32 = jnp.bfloat16, jnp.float32

    def call(kernel, *shapes, more_specs=(), more=()):
        return pl.pallas_call(
            kernel,
            in_specs=[smem, smem, anywhere] + [anywhere] * N_PIECES + list(more_specs),
            out_specs=[vmem] * len(shapes),
            out_shape=shapes,
            scratch_shapes=[
                pltpu.VMEM((2, 2, Z, q, vectors), bf),
                pltpu.VMEM((2, vectors, width), bf),
                pltpu.SemaphoreType.DMA((2, 2)),
                pltpu.SemaphoreType.DMA((2,)),
            ],
            compiler_params=params,
            cost_estimate=pl.CostEstimate(
                flops=owned * (4 * Z * q * vectors * width + 2 * Z * q * width * width),
                bytes_accessed=owned * (4 * Z * q * vectors + 2 * vectors * width + 4 * width * width),
                transcendentals=0,
            ),
        )(here, orbs, pno_maps, *pieces, *more)

    def partial(group, *kinds):
        shapes = [jax.ShapeDtypeStruct((owned, rows, width), kind) for kind in kinds]
        return call(functools.partial(partial_kernel, group), *shapes)

    far_top, far_bottom = partial(2, bf, bf)
    far_top, far_bottom = send(far_top, X_AHEAD), send(far_bottom, X_BEHIND)
    up_top, up_bottom = partial(1, f32, bf)
    up_bottom = send(up_bottom, X_AHEAD)
    down_top, down_bottom = partial(3, bf, f32)
    down_top = send(down_top, X_BEHIND)
    up_top = send((up_top + far_top.astype(f32)).astype(bf), X_AHEAD)
    down_bottom = send((down_bottom + far_bottom.astype(f32)).astype(bf), X_BEHIND)

    whole = jax.ShapeDtypeStruct((owned, width, width), f32)
    (acc,) = call(own_kernel, whole, more_specs=[smem, vmem, vmem], more=(orbital_energy, pno_energy, amplitudes))
    return pl.pallas_call(
        last_kernel,
        in_specs=[smem, vmem, vmem, vmem, vmem, vmem],
        out_specs=anywhere,
        out_shape=whole,
        scratch_shapes=[pltpu.VMEM((owned, width, width), f32), pltpu.SemaphoreType.DMA((owned,))],
        compiler_params=params,
    )(pair_class, acc, up_top, up_bottom, down_top, down_bottom)


def solution(mesh):
    return jax.shard_map(
        body,
        mesh=mesh,
        in_specs=(
            P("orb", "pair", None),
            P("orb", None, None),
            P("orb", None),
            P(("orb", "pair")),
            P(),
            P(("orb", "pair"), None),
            P(("orb", "pair"), None, None),
        ),
        out_specs=P(("orb", "pair"), None, None),
        check_vma=False,
    )
```

```python
import functools

import jax
import jax.numpy as jnp
from jax import lax
from jax.experimental import pallas as pl
from jax.experimental.pallas import tpu as pltpu
from jax.sharding import PartitionSpec as P

NSMALL = 256
AXES = ("orb", "pair")
Y, C, X, Z = 4, 2, 4, 4
VMEM = 16 * 1024 * 1024


def flat(y, c, x, z):
    return (((y % Y) * C + c) * X + x % X) * Z + z % Z


def route(hop):
    return [
        (flat(y, c, x, z), flat(*hop(y, c, x, z)))
        for y in range(Y)
        for c in range(C)
        for x in range(X)
        for z in range(Z)
    ]


Y_ROUTE = route(lambda y, c, x, z: (y + 1 - 2 * c, c, x, z))
Z_ROUTE = route(lambda y, c, x, z: (y, c, x, z + 1 - 2 * c))
Y_FAR = route(lambda y, c, x, z: (y + 2, c, x, z))
Z_FAR = route(lambda y, c, x, z: (y, c, x, z + 2))
SWAP = route(lambda y, c, x, z: (y, 1 - c, x, z))
X_AHEAD = route(lambda y, c, x, z: (y, c, x + 1 - 2 * c, z))
X_BEHIND = route(lambda y, c, x, z: (y, c, x - 1 + 2 * c, z))


def send(value, way):
    return lax.ppermute(value, AXES, way)


def after(value, *others):
    return lax.optimization_barrier((value, *others))[0]


def gather(own):
    rz2 = send(own, Z_FAR)
    other = send(own, SWAP)
    wb = jnp.stack([own[1], other[1]])
    ry2 = send(own, Y_FAR)
    srz2 = send(rz2, SWAP)
    zb = send(wb, Z_ROUTE)
    sry2 = send(ry2, SWAP)
    wa = jnp.stack([own[0], other[0]])
    ya = send(wa, Y_ROUTE)
    za = send(after(wa, ya, zb), Z_ROUTE)
    yb = send(after(wb, ya, zb), Y_ROUTE)
    sya = send(ya, SWAP)
    on_z = jnp.stack([jnp.stack([ya[0], sya[1], ry2[0]]), jnp.stack([ya[1], sya[0], sry2[0]])])
    rz3 = send(on_z, Z_ROUTE)
    srz3 = send(rz3, SWAP)
    rz5 = send(rz3[0], Z_ROUTE)
    srz5 = send(rz5, SWAP)
    szb = send(zb, SWAP)
    on_y = jnp.stack([jnp.stack([zb[0], szb[1], rz2[1]]), jnp.stack([zb[1], szb[0], srz2[1]])])
    ry3 = send(on_y, Y_ROUTE)
    sry3 = send(ry3, SWAP)
    leaf = send(jnp.stack([after(yb, on_z, on_y), za]), SWAP)
    ry5 = send(ry3[0], Y_ROUTE)
    sry5 = send(ry5, SWAP)
    return wa, wb, ya, sya, yb, za, leaf, zb, szb, ry2, sry2, rz2, srz2, rz3, srz3, rz5, srz5, ry3, sry3, ry5, sry5


FLIP = (0, 2, 1, 3)
N_PIECES = 21


def fetch(pieces, dy, l, dc, dst, sem):
    wa, wb, ya, sya, yb, za, leaf, zb, szb, ry2, sry2, rz2, srz2, rz3, srz3, rz5, srz5, ry3, sry3, ry5, sry5 = pieces
    syb, sza = leaf.at[0], leaf.at[1]
    def copy(src, dz):
        pltpu.make_async_copy(src, dst.at[dz], sem).start()

    flipped = jnp.where(dy == 3, 3, 3 - dy)

    @pl.when((l == 0) & (dy == 0))
    def _():
        copy(wa.at[dc], 0)
        copy(za.at[dc], 1)
        copy(sza.at[1 - dc], 2)

    @pl.when((l == 1) & (dy == 0))
    def _():
        copy(wb.at[dc], 0)
        copy(zb.at[dc], 1)
        copy(szb.at[1 - dc], 2)

    @pl.when((dy == 0) & (dc == 0))
    def _():
        copy(rz2.at[l], 3)

    @pl.when((dy == 0) & (dc == 1))
    def _():
        copy(srz2.at[l], 3)

    @pl.when((dy == 3) & (dc == 0))
    def _():
        copy(ry2.at[l], 0)

    @pl.when((dy == 3) & (dc == 1))
    def _():
        copy(sry2.at[l], 0)

    @pl.when((l == 0) & (dy != 0))
    def _():
        @pl.when(dy == 1)
        def _():
            copy(ya.at[dc], 0)

        @pl.when(dy == 2)
        def _():
            copy(sya.at[1 - dc], 0)

        copy(rz3.at[dc, dy - 1], 1)
        copy(srz3.at[1 - dc, flipped - 1], 2)

        @pl.when(dc == 0)
        def _():
            copy(rz5.at[dy - 1], 3)

        @pl.when(dc == 1)
        def _():
            copy(srz5.at[flipped - 1], 3)

    @pl.when((l == 1) & (dy == 1))
    def _():
        copy(yb.at[dc], 0)
        for dz in (1, 2, 3):
            copy(ry3.at[dc, dz - 1], dz)

    @pl.when((l == 1) & (dy == 2))
    def _():
        copy(syb.at[1 - dc], 0)
        for dz in (1, 2, 3):
            copy(sry3.at[1 - dc, FLIP[dz] - 1], dz)

    @pl.when((l == 1) & (dy == 3))
    def _():
        @pl.when(dc == 0)
        def _():
            for dz in (1, 2, 3):
                copy(ry5.at[dz - 1], dz)

        @pl.when(dc == 1)
        def _():
            for dz in (1, 2, 3):
                copy(sry5.at[FLIP[dz] - 1], dz)


def sweep(group, here, orbs, maps, pieces, scratch, act):
    rows_of, dmaps, row_sems, map_sems = scratch
    pairs = orbs.shape[1] // (X * Z)

    def start(p):
        row = here[2 + group] + p
        slot = lax.rem(p, 2)
        pltpu.make_async_copy(maps.at[row], dmaps.at[slot], map_sems.at[slot]).start()

        @pl.loop(0, 2)
        def _(side):
            k = orbs[side, row]
            away = lax.rem(k // (2 * C) + Y - here[0], Y)
            near = jnp.where((away == 3) == (here[1] == 0), 1, 2)
            dy = jnp.where(away == 0, 0, jnp.where(away == 2, 3, near))
            dc = lax.rem(k // 2 + here[1], 2)
            fetch(pieces, dy, lax.rem(k, 2), dc, rows_of.at[slot, side], row_sems.at[slot, side])

    @pl.loop(0, pairs + 1)
    def _(n):
        @pl.when(n < pairs)
        def _():
            start(n)

        @pl.when(n > 0)
        def _():
            p = n - 1
            slot = lax.rem(p, 2)
            pltpu.make_async_copy(dmaps.at[slot], dmaps.at[slot], map_sems.at[slot]).wait()
            for side in range(2):
                rows = rows_of.at[slot, side]
                pltpu.make_async_copy(rows, rows, row_sems.at[slot, side]).wait()
            q, v = rows_of.shape[2] * rows_of.shape[3], rows_of.shape[4]
            act(p, dmaps[slot], *(rows_of[slot, side].reshape(q, v) for side in range(2)))


def left_t(dmap, rows):
    product = lax.dot_general(dmap, rows, (((0,), (1,)), ((), ())), preferred_element_type=jnp.float32)
    return product.astype(jnp.bfloat16)


def right(dmap, rows):
    return jnp.dot(rows, dmap, preferred_element_type=jnp.float32).astype(jnp.bfloat16)


def meet(lt, r):
    return jnp.dot(lt, r, preferred_element_type=jnp.float32)


def partial_kernel(group, here, orbs, maps, *refs):
    pieces, (top, bottom), scratch = refs[:N_PIECES], refs[N_PIECES : N_PIECES + 2], refs[N_PIECES + 2 :]
    rows = top.shape[1]

    def act(p, dmap, left_rows, right_rows):
        exchange = meet(left_t(dmap, left_rows), right(dmap, right_rows))
        top[p] = exchange[:rows].astype(top.dtype)
        bottom[p] = exchange[rows:].astype(bottom.dtype)

    sweep(group, here, orbs, maps, pieces, scratch, act)


def own_kernel(here, orbs, maps, *refs):
    pieces, (orbital_energy, energy, amp, out) = refs[:N_PIECES], refs[N_PIECES : N_PIECES + 4]

    def act(p, dmap, left_rows, right_rows):
        row = here[2] + p
        occupied = orbital_energy[orbs[0, row]] + orbital_energy[orbs[1, row]]
        exchange = meet(left_t(dmap, left_rows), right(dmap, right_rows))
        along = jnp.broadcast_to(energy[pl.ds(p, 1), :], exchange.shape)
        out[p] = exchange + (along.T + along - occupied) * amp[p]

    sweep(0, here, orbs, maps, pieces, refs[N_PIECES + 4 :], act)


def last_kernel(kinds, acc, up_top, up_bottom, down_top, down_bottom, out, staged, sems):
    owned, rows, width = up_top.shape
    b = lax.broadcasted_iota(jnp.int32, (rows, width), 1)
    copies = []
    for p in range(owned):
        size = NSMALL + kinds[p] * (width - NSMALL)
        for begin, near, late in ((0, down_top, up_top), (rows, up_bottom, down_bottom)):
            a = lax.broadcasted_iota(jnp.int32, (rows, width), 0) + begin
            part = pl.ds(begin, rows)
            total = acc[p, part] + near[p].astype(jnp.float32) + late[p].astype(jnp.float32)
            staged[p, part] = jnp.where((a < size) & (b < size), total, 0.0)
        copies.append(pltpu.make_async_copy(staged.at[p], out.at[p], sems.at[p]))
        copies[-1].start()
    for copy in copies:
        copy.wait()


def body(integrals, pno_maps, pair_orbs, pair_class, orbital_energy, pno_energy, amplitudes):
    local_pairs, vectors, width = pno_maps.shape
    owned = local_pairs // (X * Z)
    rows = width // 2
    orb, spot = lax.axis_index("orb"), lax.axis_index("pair")
    x, z = spot // Z, spot % Z
    c = orb % C
    ahead = 1 - 2 * c
    here = jnp.stack([orb // C, c] + [owned * ((x + k * ahead + 4 * X) % X * Z + z) for k in range(X)]).astype(jnp.int32)
    orbs = pair_orbs.T
    pno_maps = pltpu.with_memory_space_constraint(pno_maps, pltpu.HBM)

    pieces = [pltpu.with_memory_space_constraint(piece, pltpu.HBM) for piece in gather(integrals)]
    q = integrals.shape[1]
    smem, vmem, anywhere = (pl.BlockSpec(memory_space=m) for m in (pltpu.SMEM, pltpu.VMEM, pl.ANY))
    params = pltpu.CompilerParams(vmem_limit_bytes=VMEM)
    bf, f32 = jnp.bfloat16, jnp.float32

    def call(kernel, *shapes, more_specs=(), more=()):
        return pl.pallas_call(
            kernel,
            in_specs=[smem, smem, anywhere] + [anywhere] * N_PIECES + list(more_specs),
            out_specs=[vmem] * len(shapes),
            out_shape=shapes,
            scratch_shapes=[
                pltpu.VMEM((2, 2, Z, q, vectors), bf),
                pltpu.VMEM((2, vectors, width), bf),
                pltpu.SemaphoreType.DMA((2, 2)),
                pltpu.SemaphoreType.DMA((2,)),
            ],
            compiler_params=params,
            cost_estimate=pl.CostEstimate(
                flops=10 * owned * (4 * Z * q * vectors * width + 2 * Z * q * width * width),
                bytes_accessed=10 * owned * (4 * Z * q * vectors + 2 * vectors * width + 4 * width * width),
                transcendentals=0,
            ),
        )(here, orbs, pno_maps, *pieces, *more)

    def partial(group, *kinds):
        shapes = [jax.ShapeDtypeStruct((owned, rows, width), kind) for kind in kinds]
        return call(functools.partial(partial_kernel, group), *shapes)

    far_top, far_bottom = partial(2, bf, bf)
    far_top, far_bottom = send(far_top, X_AHEAD), send(far_bottom, X_BEHIND)
    up_top, up_bottom = partial(1, f32, bf)
    up_bottom = send(up_bottom, X_AHEAD)
    down_top, down_bottom = partial(3, bf, f32)
    down_top = send(down_top, X_BEHIND)
    up_top = send((up_top + far_top.astype(f32)).astype(bf), X_AHEAD)
    down_bottom = send((down_bottom + far_bottom.astype(f32)).astype(bf), X_BEHIND)

    whole = jax.ShapeDtypeStruct((owned, width, width), f32)
    (acc,) = call(own_kernel, whole, more_specs=[smem, vmem, vmem], more=(orbital_energy, pno_energy, amplitudes))
    return pl.pallas_call(
        last_kernel,
        in_specs=[smem, vmem, vmem, vmem, vmem, vmem],
        out_specs=anywhere,
        out_shape=whole,
        scratch_shapes=[pltpu.VMEM((owned, width, width), f32), pltpu.SemaphoreType.DMA((owned,))],
        compiler_params=params,
    )(pair_class, acc, up_top, up_bottom, down_top, down_bottom)


def solution(mesh):
    return jax.shard_map(
        body,
        mesh=mesh,
        in_specs=(
            P("orb", "pair", None),
            P("orb", None, None),
            P("orb", None),
            P(("orb", "pair")),
            P(),
            P(("orb", "pair"), None),
            P(("orb", "pair"), None, None),
        ),
        out_specs=P(("orb", "pair"), None, None),
        check_vma=False,
    )
```

```python
import functools

import jax
import jax.numpy as jnp
from jax import lax
from jax.experimental import pallas as pl
from jax.experimental.pallas import tpu as pltpu
from jax.sharding import PartitionSpec as P

NSMALL = 256
AXES = ("orb", "pair")
Y, C, X, Z = 4, 2, 4, 4
VMEM = 16 * 1024 * 1024


def flat(y, c, x, z):
    return (((y % Y) * C + c) * X + x % X) * Z + z % Z


def route(hop):
    return [
        (flat(y, c, x, z), flat(*hop(y, c, x, z)))
        for y in range(Y)
        for c in range(C)
        for x in range(X)
        for z in range(Z)
    ]


Y_ROUTE = route(lambda y, c, x, z: (y + 1 - 2 * c, c, x, z))
Z_ROUTE = route(lambda y, c, x, z: (y, c, x, z + 1 - 2 * c))
Y_FAR = route(lambda y, c, x, z: (y + 2, c, x, z))
Z_FAR = route(lambda y, c, x, z: (y, c, x, z + 2))
SWAP = route(lambda y, c, x, z: (y, 1 - c, x, z))
X_AHEAD = route(lambda y, c, x, z: (y, c, x + 1 - 2 * c, z))
X_BEHIND = route(lambda y, c, x, z: (y, c, x - 1 + 2 * c, z))


def send(value, way):
    return lax.ppermute(value, AXES, way)


def after(value, *others):
    return lax.optimization_barrier((value, *others))[0]


def gather(own):
    rz2 = send(own, Z_FAR)
    other = send(own, SWAP)
    wb = jnp.stack([own[1], other[1]])
    ry2 = send(own, Y_FAR)
    srz2 = send(rz2, SWAP)
    zb = send(wb, Z_ROUTE)
    sry2 = send(ry2, SWAP)
    wa = jnp.stack([own[0], other[0]])
    ya = send(wa, Y_ROUTE)
    za = send(after(wa, ya, zb), Z_ROUTE)
    yb = send(after(wb, ya, zb), Y_ROUTE)
    sya = send(ya, SWAP)
    on_z = jnp.stack([jnp.stack([ya[0], sya[1], ry2[0]]), jnp.stack([ya[1], sya[0], sry2[0]])])
    rz3 = send(on_z, Z_ROUTE)
    srz3 = send(rz3, SWAP)
    rz5 = send(rz3[0], Z_ROUTE)
    srz5 = send(rz5, SWAP)
    szb = send(zb, SWAP)
    on_y = jnp.stack([jnp.stack([zb[0], szb[1], rz2[1]]), jnp.stack([zb[1], szb[0], srz2[1]])])
    ry3 = send(on_y, Y_ROUTE)
    sry3 = send(ry3, SWAP)
    leaf = send(jnp.stack([after(yb, on_z, on_y), za]), SWAP)
    ry5 = send(ry3[0], Y_ROUTE)
    sry5 = send(ry5, SWAP)
    return wa, wb, ya, sya, yb, za, leaf, zb, szb, ry2, sry2, rz2, srz2, rz3, srz3, rz5, srz5, ry3, sry3, ry5, sry5


FLIP = (0, 2, 1, 3)
N_PIECES = 21


def fetch(pieces, dy, l, dc, dst, sem):
    wa, wb, ya, sya, yb, za, leaf, zb, szb, ry2, sry2, rz2, srz2, rz3, srz3, rz5, srz5, ry3, sry3, ry5, sry5 = pieces
    syb, sza = leaf.at[0], leaf.at[1]
    def copy(src, dz):
        pltpu.make_async_copy(src, dst.at[dz], sem).start()

    flipped = jnp.where(dy == 3, 3, 3 - dy)

    @pl.when((l == 0) & (dy == 0))
    def _():
        copy(wa.at[dc], 0)
        copy(za.at[dc], 1)
        copy(sza.at[1 - dc], 2)

    @pl.when((l == 1) & (dy == 0))
    def _():
        copy(wb.at[dc], 0)
        copy(zb.at[dc], 1)
        copy(szb.at[1 - dc], 2)

    @pl.when((dy == 0) & (dc == 0))
    def _():
        copy(rz2.at[l], 3)

    @pl.when((dy == 0) & (dc == 1))
    def _():
        copy(srz2.at[l], 3)

    @pl.when((dy == 3) & (dc == 0))
    def _():
        copy(ry2.at[l], 0)

    @pl.when((dy == 3) & (dc == 1))
    def _():
        copy(sry2.at[l], 0)

    @pl.when((l == 0) & (dy != 0))
    def _():
        @pl.when(dy == 1)
        def _():
            copy(ya.at[dc], 0)

        @pl.when(dy == 2)
        def _():
            copy(sya.at[1 - dc], 0)

        copy(rz3.at[dc, dy - 1], 1)
        copy(srz3.at[1 - dc, flipped - 1], 2)

        @pl.when(dc == 0)
        def _():
            copy(rz5.at[dy - 1], 3)

        @pl.when(dc == 1)
        def _():
            copy(srz5.at[flipped - 1], 3)

    @pl.when((l == 1) & (dy == 1))
    def _():
        copy(yb.at[dc], 0)
        for dz in (1, 2, 3):
            copy(ry3.at[dc, dz - 1], dz)

    @pl.when((l == 1) & (dy == 2))
    def _():
        copy(syb.at[1 - dc], 0)
        for dz in (1, 2, 3):
            copy(sry3.at[1 - dc, FLIP[dz] - 1], dz)

    @pl.when((l == 1) & (dy == 3))
    def _():
        @pl.when(dc == 0)
        def _():
            for dz in (1, 2, 3):
                copy(ry5.at[dz - 1], dz)

        @pl.when(dc == 1)
        def _():
            for dz in (1, 2, 3):
                copy(sry5.at[FLIP[dz] - 1], dz)


def sweep(group, here, orbs, maps, pieces, scratch, act):
    rows_of, dmaps, row_sems, map_sems = scratch
    pairs = orbs.shape[1] // (X * Z)

    def start(p):
        row = here[2 + group] + p
        slot = lax.rem(p, 2)
        pltpu.make_async_copy(maps.at[row], dmaps.at[slot], map_sems.at[slot]).start()

        @pl.loop(0, 2)
        def _(side):
            k = orbs[side, row]
            away = lax.rem(k // (2 * C) + Y - here[0], Y)
            near = jnp.where((away == 3) == (here[1] == 0), 1, 2)
            dy = jnp.where(away == 0, 0, jnp.where(away == 2, 3, near))
            dc = lax.rem(k // 2 + here[1], 2)
            fetch(pieces, dy, lax.rem(k, 2), dc, rows_of.at[slot, side], row_sems.at[slot, side])

    @pl.loop(0, pairs + 1)
    def _(n):
        @pl.when(n < pairs)
        def _():
            start(n)

        @pl.when(n > 0)
        def _():
            p = n - 1
            slot = lax.rem(p, 2)
            pltpu.make_async_copy(dmaps.at[slot], dmaps.at[slot], map_sems.at[slot]).wait()
            for side in range(2):
                rows = rows_of.at[slot, side]
                pltpu.make_async_copy(rows, rows, row_sems.at[slot, side]).wait()
            q, v = rows_of.shape[2] * rows_of.shape[3], rows_of.shape[4]
            act(p, dmaps[slot], *(rows_of[slot, side].reshape(q, v) for side in range(2)))


def left_t(dmap, rows):
    product = lax.dot_general(dmap, rows, (((0,), (1,)), ((), ())), preferred_element_type=jnp.float32)
    return product.astype(jnp.bfloat16)


def right(dmap, rows):
    return jnp.dot(rows, dmap, preferred_element_type=jnp.float32).astype(jnp.bfloat16)


def meet(lt, r):
    return jnp.dot(lt, r, preferred_element_type=jnp.float32)


def partial_kernel(group, here, orbs, maps, *refs):
    pieces, (top, bottom), scratch = refs[:N_PIECES], refs[N_PIECES : N_PIECES + 2], refs[N_PIECES + 2 :]
    rows = top.shape[1]

    def act(p, dmap, left_rows, right_rows):
        exchange = meet(left_t(dmap, left_rows), right(dmap, right_rows))
        top[p] = exchange[:rows].astype(top.dtype)
        bottom[p] = exchange[rows:].astype(bottom.dtype)

    sweep(group, here, orbs, maps, pieces, scratch, act)


def own_kernel(here, orbs, maps, *refs):
    pieces, (orbital_energy, energy, amp, out) = refs[:N_PIECES], refs[N_PIECES : N_PIECES + 4]

    def act(p, dmap, left_rows, right_rows):
        row = here[2] + p
        occupied = orbital_energy[orbs[0, row]] + orbital_energy[orbs[1, row]]
        exchange = meet(left_t(dmap, left_rows), right(dmap, right_rows))
        along = jnp.broadcast_to(energy[pl.ds(p, 1), :], exchange.shape)
        out[p] = exchange + (along.T + along - occupied) * amp[p]

    sweep(0, here, orbs, maps, pieces, refs[N_PIECES + 4 :], act)


def last_kernel(kinds, acc, up_top, up_bottom, down_top, down_bottom, out, staged, sems):
    owned, rows, width = up_top.shape
    b = lax.broadcasted_iota(jnp.int32, (rows, width), 1)
    copies = []
    for p in range(owned):
        size = NSMALL + kinds[p] * (width - NSMALL)
        for begin, near, late in ((0, down_top, up_top), (rows, up_bottom, down_bottom)):
            a = lax.broadcasted_iota(jnp.int32, (rows, width), 0) + begin
            part = pl.ds(begin, rows)
            total = acc[p, part] + near[p].astype(jnp.float32) + late[p].astype(jnp.float32)
            staged[p, part] = jnp.where((a < size) & (b < size), total, 0.0)
            for i in range(2):
                piece = pl.ds(begin + i * (rows // 2), rows // 2)
                sem = sems.at[p, 2 * (begin // rows) + i]
                copies.append(pltpu.make_async_copy(staged.at[p, piece], out.at[p, piece], sem))
                copies[-1].start()
    for copy in copies:
        copy.wait()


def body(integrals, pno_maps, pair_orbs, pair_class, orbital_energy, pno_energy, amplitudes):
    local_pairs, vectors, width = pno_maps.shape
    owned = local_pairs // (X * Z)
    rows = width // 2
    orb, spot = lax.axis_index("orb"), lax.axis_index("pair")
    x, z = spot // Z, spot % Z
    c = orb % C
    ahead = 1 - 2 * c
    here = jnp.stack([orb // C, c] + [owned * ((x + k * ahead + 4 * X) % X * Z + z) for k in range(X)]).astype(jnp.int32)
    orbs = pair_orbs.T
    pno_maps = pltpu.with_memory_space_constraint(pno_maps, pltpu.HBM)

    pieces = [pltpu.with_memory_space_constraint(piece, pltpu.HBM) for piece in gather(integrals)]
    q = integrals.shape[1]
    smem, vmem, anywhere = (pl.BlockSpec(memory_space=m) for m in (pltpu.SMEM, pltpu.VMEM, pl.ANY))
    params = pltpu.CompilerParams(vmem_limit_bytes=VMEM)
    bf, f32 = jnp.bfloat16, jnp.float32

    def call(kernel, *shapes, more_specs=(), more=()):
        return pl.pallas_call(
            kernel,
            in_specs=[smem, smem, anywhere] + [anywhere] * N_PIECES + list(more_specs),
            out_specs=[vmem] * len(shapes),
            out_shape=shapes,
            scratch_shapes=[
                pltpu.VMEM((2, 2, Z, q, vectors), bf),
                pltpu.VMEM((2, vectors, width), bf),
                pltpu.SemaphoreType.DMA((2, 2)),
                pltpu.SemaphoreType.DMA((2,)),
            ],
            compiler_params=params,
            cost_estimate=pl.CostEstimate(
                flops=10 * owned * (4 * Z * q * vectors * width + 2 * Z * q * width * width),
                bytes_accessed=10 * owned * (4 * Z * q * vectors + 2 * vectors * width + 4 * width * width),
                transcendentals=0,
            ),
        )(here, orbs, pno_maps, *pieces, *more)

    def partial(group, *kinds):
        shapes = [jax.ShapeDtypeStruct((owned, rows, width), kind) for kind in kinds]
        return call(functools.partial(partial_kernel, group), *shapes)

    far_top, far_bottom = partial(2, bf, bf)
    far_top, far_bottom = send(far_top, X_AHEAD), send(far_bottom, X_BEHIND)
    up_top, up_bottom = partial(1, f32, bf)
    up_bottom = send(up_bottom, X_AHEAD)
    down_top, down_bottom = partial(3, bf, f32)
    down_top = send(down_top, X_BEHIND)
    up_top = send((up_top + far_top.astype(f32)).astype(bf), X_AHEAD)
    down_bottom = send((down_bottom + far_bottom.astype(f32)).astype(bf), X_BEHIND)

    whole = jax.ShapeDtypeStruct((owned, width, width), f32)
    (acc,) = call(own_kernel, whole, more_specs=[smem, vmem, vmem], more=(orbital_energy, pno_energy, amplitudes))
    return pl.pallas_call(
        last_kernel,
        in_specs=[smem, vmem, vmem, vmem, vmem, vmem],
        out_specs=anywhere,
        out_shape=whole,
        scratch_shapes=[pltpu.VMEM((owned, width, width), f32), pltpu.SemaphoreType.DMA((owned, 4))],
        compiler_params=params,
    )(pair_class, acc, up_top, up_bottom, down_top, down_bottom)


def solution(mesh):
    return jax.shard_map(
        body,
        mesh=mesh,
        in_specs=(
            P("orb", "pair", None),
            P("orb", None, None),
            P("orb", None),
            P(("orb", "pair")),
            P(),
            P(("orb", "pair"), None),
            P(("orb", "pair"), None, None),
        ),
        out_specs=P(("orb", "pair"), None, None),
        check_vma=False,
    )
```
